32 devices in a mesh: box: 8 (over z, x), dir: 4 (over y, core).
Axes of the slice: x: 2, y: 2, z: 4, core: 2. Of those that a mesh axis runs over, the one named last changes fastest.
Arguments:
- currents: bfloat16 [2, 768, 128, 256], P(None, ('box', 'dir')), may hold values from -6 to 6
- near_tiles: bfloat16 [768, 9, 2, 128, 128], P(('box', 'dir')), may hold values from -0.125 to 0.125
- near_index: int32 [768, 9], P(('box', 'dir')), may hold values from 0 to 767, as said below
- near_count: int32 [768], P(('box', 'dir')), may hold values from 2 to 9
- radiate: bfloat16 [768, 2, 128, 128], P(('box', 'dir')), may hold values from -0.375 to 0.375
- receive: bfloat16 [768, 2, 128, 128], P(('box', 'dir')), may hold values from -0.375 to 0.375
- interp: bfloat16 [512, 128], replicated, may hold values from -0.1875 to 0.1875
- shift_angle: float32 [8, 512], replicated, may hold values from -3.140625 to 3.140625
- far_index: int32 [96, 48], replicated, may hold values from 0 to 95, as said below
- far_count: int32 [96], replicated, may hold values from 12 to 48
- trans_index: int32 [96, 48], replicated, may hold values from 0 to 315
- translators: float32 [316, 2, 512], P(None, None, ('box', 'dir')), may hold values from -0.625 to 0.625
Outputs:
- response: bfloat16 [2, 768, 128, 256], P(None, ('box', 'dir'))
The draws below stay inside these ranges and needn't reach their ends.
Inputs may be any that keep to these rules, and one draw needn't show every extreme that they name: `near_index`: slot 0 of box b is b itself; every entry lies within 12 of its own box's index. `far_index`: no parent box lists itself.
All inputs are finite; a program needn't handle non-finite values.
Results may differ from the reference program's by a relative error of at most 0.007.
Values may be sent and summed in bfloat16 or wider, within the bound.
A program may use at most 256 MiB of HBM per device.

```python
import jax
import jax.numpy as jnp
from jax import lax

P_SIZE = 128
K_A = 128
K_B = 512
NEAR = 9
FAR = 48
NOFF = 316
BOX_DEV = 24
NRHS = 256
NB = 768
PARENTS = 96
REACH = 12


def draw_near_index(key, part):
    key = jax.random.fold_in(key, 11)
    own = jnp.arange(NB, dtype=jnp.int32)[:, None]
    offset = jax.random.randint(key, (NB, NEAR), -REACH, REACH + 1, dtype=jnp.int32)
    chosen = jnp.clip(own + offset, 0, NB - 1)
    slot_ids = jnp.arange(NEAR, dtype=jnp.int32)[None, :]
    return jnp.where(slot_ids == 0, own, chosen).astype(jnp.int32)


def draw_far_index(key, part):
    key = jax.random.fold_in(key, 23)
    own = jnp.arange(PARENTS, dtype=jnp.int32)[:, None]
    offset = jax.random.randint(key, (PARENTS, FAR), 1, PARENTS, dtype=jnp.int32)
    return ((own + offset) % PARENTS).astype(jnp.int32)


def plant(drawn, stream_key, low, top_value):
    dims = drawn.shape
    place = [jax.random.randint(jax.random.fold_in(stream_key, axis), (), 0, dims[axis]) for axis in range(len(dims))]
    drawn = drawn.at[tuple(place)].set(low)
    longest = dims.index(max(dims))
    place[longest] = (place[longest] + 1) % dims[longest]
    return drawn.at[tuple(place)].set(top_value)


def block_levels(rng, extent, split, least, high):
    gain = 1.0
    for position, parts in split:
        heights = jax.random.uniform(jax.random.fold_in(jax.random.fold_in(rng, 6), position), (parts,), jnp.float32, least / len(split), high / len(split))
        gain = gain * jnp.repeat(jnp.exp(heights), extent[position] // parts).reshape((-1,) + (1,) * (len(extent) - 1 - position))
    return gain


def bell_draw(stream_key, dims, scale, bound, split=(), held_as=jnp.bfloat16):
    array = scale * jax.random.normal(stream_key, dims, jnp.float32)
    if split:
        array = array * block_levels(stream_key, dims, split, -0.22, 0.18)
    return jnp.clip(array, -bound, bound).astype(held_as)


def setup_inputs(seed: int = 0) -> dict:
    splits = jax.random.split(jax.random.key(seed), 13)
    currents = bell_draw(splits[0], (2, NB, P_SIZE, NRHS), 1.0, 6.0, ((1, 32),))
    near_tiles = bell_draw(splits[1], (NB, NEAR, 2, P_SIZE, P_SIZE), (2 * P_SIZE * NEAR) ** -0.5, 0.125, ((0, 32),))
    near_index = draw_near_index(jax.random.fold_in(splits[12], 71), 0)
    near_count = plant(jax.random.randint(splits[3], (NB,), 2, NEAR + 1), jax.random.fold_in(splits[3], 1), 2, NEAR).astype(jnp.int32)
    radiate = bell_draw(splits[4], (NB, 2, K_A, P_SIZE), (2 * P_SIZE) ** -0.5, 0.375, ((0, 32),))
    receive = bell_draw(splits[5], (NB, 2, P_SIZE, K_A), (2 * K_A) ** -0.5, 0.375, ((0, 32),))
    interp = bell_draw(splits[6], (K_B, K_A), (8 * K_A) ** -0.5, 0.1875)
    shift_angle = jnp.clip(jax.random.uniform(splits[7], (8, K_B), jnp.float32, -3.140625, 3.140625), -3.140625, 3.140625)
    far_index = draw_far_index(jax.random.fold_in(splits[12], 71), 0)
    far_count = plant(jax.random.randint(splits[9], (PARENTS,), max(1, FAR // 4), FAR + 1), jax.random.fold_in(splits[9], 1), max(1, FAR // 4), FAR).astype(jnp.int32)
    trans_index = plant(jax.random.randint(splits[10], (PARENTS, FAR), 0, NOFF), jax.random.fold_in(splits[10], 1), 0, NOFF - 1).astype(jnp.int32)
    translators = bell_draw(splits[11], (NOFF, 2, K_B), (2 * FAR) ** -0.5, 0.625, ((2, 32),), jnp.float32)
    return dict(currents=currents, near_tiles=near_tiles, near_index=near_index, near_count=near_count, radiate=radiate, receive=receive, interp=interp, shift_angle=shift_angle, far_index=far_index, far_count=far_count, trans_index=trans_index, translators=translators)


def complex_product(form, mat_real, mat_imag, vec_real, vec_imag):
    real_part = jnp.einsum(form, mat_real, vec_real) - jnp.einsum(form, mat_imag, vec_imag)
    imag_part = jnp.einsum(form, mat_real, vec_imag) + jnp.einsum(form, mat_imag, vec_real)
    return jnp.stack([real_part, imag_part])


def translate(patterns, far_index, far_count, trans_index, translators, block_size):
    total_boxes, slot_count = far_index.shape
    slot_ids = jnp.arange(slot_count, dtype=jnp.int32)

    def one_block(inputs):
        partner, counts, offsets = inputs
        live_mask = (slot_ids[None, :] < counts[:, None]).astype(jnp.float32)
        factor = translators[offsets] * live_mask[:, :, None, None]
        sources = jnp.take(patterns, partner, axis=1).astype(jnp.float32)
        real_part = jnp.sum(factor[:, :, 0, :, None] * sources[0] - factor[:, :, 1, :, None] * sources[1], axis=1)
        imag_part = jnp.sum(factor[:, :, 1, :, None] * sources[0] + factor[:, :, 0, :, None] * sources[1], axis=1)
        return jnp.stack([real_part, imag_part]).astype(jnp.bfloat16)

    groups = total_boxes // block_size
    result = lax.map(one_block, (far_index.reshape(groups, block_size, slot_count),
                                 far_count.reshape(groups, block_size),
                                 trans_index.reshape(groups, block_size, slot_count)))
    return jnp.transpose(result, (1, 0, 2, 3, 4)).reshape(2, total_boxes, patterns.shape[2], patterns.shape[3])


def reference(currents, near_tiles, near_index, near_count, radiate, receive, interp, shift_angle,
              far_index, far_count, trans_index, translators):
    groups = NB // BOX_DEV
    kids = BOX_DEV // 8
    cosine = jnp.cos(shift_angle)[None, :, :, None]
    sine = jnp.sin(shift_angle)[None, :, :, None]
    interp_wide = interp.astype(jnp.float32)

    def upward(group):
        start = group * BOX_DEV
        block_currents = lax.dynamic_slice_in_dim(currents, start, BOX_DEV, 1).astype(jnp.float32)
        block_radiate = lax.dynamic_slice_in_dim(radiate, start, BOX_DEV, 0).astype(jnp.float32)
        leaf = complex_product("bkp,bpr->bkr", block_radiate[:, 0], block_radiate[:, 1],
                               block_currents[0], block_currents[1]).astype(jnp.bfloat16)
        spread = jnp.einsum("jk,sbkr->sbjr", interp_wide, leaf.astype(jnp.float32))
        spread = spread.reshape(2, kids, 8, K_B, NRHS)
        real_part = jnp.sum(cosine * spread[0] - sine * spread[1], axis=1)
        imag_part = jnp.sum(sine * spread[0] + cosine * spread[1], axis=1)
        return jnp.stack([real_part, imag_part]).astype(jnp.bfloat16)

    parent = lax.map(upward, jnp.arange(groups, dtype=jnp.int32))
    parent = jnp.transpose(parent, (1, 0, 2, 3, 4)).reshape(2, PARENTS, K_B, NRHS)
    incoming = translate(parent, far_index, far_count, trans_index, translators, 1)
    slot_ids = jnp.arange(NEAR, dtype=jnp.int32)

    def downward(group):
        start = group * BOX_DEV
        block_in = lax.dynamic_slice_in_dim(incoming, group * kids, kids, 1).astype(jnp.float32)
        in_real = block_in[0][:, None]
        in_imag = block_in[1][:, None]
        phased = jnp.stack([cosine * in_real + sine * in_imag,
                            cosine * in_imag - sine * in_real]).astype(jnp.bfloat16)
        phased = phased.reshape(2, BOX_DEV, K_B, NRHS)
        arriving = jnp.einsum("jk,sbjr->sbkr", interp_wide, phased.astype(jnp.float32)).astype(jnp.bfloat16)
        block_receive = lax.dynamic_slice_in_dim(receive, start, BOX_DEV, 0).astype(jnp.float32)
        arriving = arriving.astype(jnp.float32)
        far_field = complex_product("bpk,bkr->bpr", block_receive[:, 0], block_receive[:, 1],
                                    arriving[0], arriving[1])
        block_index = lax.dynamic_slice_in_dim(near_index, start, BOX_DEV, 0)
        block_count = lax.dynamic_slice_in_dim(near_count, start, BOX_DEV, 0)
        live_mask = (slot_ids[None, :] < block_count[:, None]).astype(jnp.float32)
        sources = jnp.take(currents, block_index, axis=1).astype(jnp.float32) * live_mask[None, :, :, None, None]
        tiles = lax.dynamic_slice_in_dim(near_tiles, start, BOX_DEV, 0).astype(jnp.float32)
        near_field = complex_product("bspq,bsqr->bpr", tiles[:, :, 0], tiles[:, :, 1], sources[0], sources[1])
        return (near_field + far_field).astype(jnp.bfloat16)

    response = lax.map(downward, jnp.arange(groups, dtype=jnp.int32))
    return jnp.transpose(response, (1, 0, 2, 3, 4)).reshape(2, NB, P_SIZE, NRHS)
```

```python
import jax
import jax.numpy as jnp
from jax import lax
from jax.experimental import pallas as pl
from jax.experimental.pallas import tpu as pltpu
from jax.sharding import PartitionSpec as P

AXES = ("box", "dir")
VMEM_BYTES = 48 * 1024 * 1024


def passed_along(value, axis, by):
    peers = lax.axis_size(axis)
    pairs = [(i, i + by) for i in range(peers) if 0 <= i + by < peers]
    return lax.ppermute(value, axis, pairs)


def complex_matrix(real, imag):
    top = jnp.concatenate([real, -imag], axis=1)
    bottom = jnp.concatenate([imag, real], axis=1)
    return jnp.concatenate([top, bottom], axis=0)


def dot(left, right):
    return jnp.dot(left, right, preferred_element_type=jnp.float32)


def upward(currents, radiate, interp, cosine, sine, parts):
    _, boxes, unknowns, columns = currents.shape
    parents = boxes // 8
    directions, leaf_dirs = interp.shape
    share = directions // parts
    half = directions // 2
    split = share % 16 == 0
    width = 2 * leaf_dirs
    currents = currents.reshape(2, parents, 8, unknowns, columns)
    radiate = radiate.reshape(parents, 8, 2, leaf_dirs, unknowns)

    def body(cur_ref, rad_ref, interp_ref, cos_ref, sin_ref, out_ref, leaf_ref, shift_ref):
        step = pl.program_id(0)

        @pl.when(step == 0)
        def _():
            wide = interp_ref[...].astype(jnp.float32)
            for c in range(8):
                real = (wide * cos_ref[:, c : c + 1]).astype(jnp.bfloat16)
                imag = (wide * sin_ref[:, c : c + 1]).astype(jnp.bfloat16)
                shift_ref[c] = complex_matrix(real, imag)

        @pl.when(step < 8)
        def _():
            rows = pl.ds(pl.multiple_of(step * width, width), width)
            for parent in range(parents):
                mat = complex_matrix(rad_ref[parent, 0, 0], rad_ref[parent, 0, 1])
                vec = jnp.concatenate([cur_ref[0, parent, 0], cur_ref[1, parent, 0]], axis=0)
                leaf = dot(mat, vec).astype(jnp.bfloat16)
                leaf_ref[rows, parent * columns : (parent + 1) * columns] = leaf
        @pl.when(step >= 8)
        def _():
            quarter = step - 8
            rows = pl.ds(pl.multiple_of(quarter * half, half), half)
            mat = jnp.concatenate([shift_ref[c, rows, :] for c in range(8)], axis=1)
            result = dot(mat, leaf_ref[...]).astype(jnp.bfloat16)
            for parent in range(parents):
                piece = result[:, parent * columns : (parent + 1) * columns]
                if split:
                    out_ref[:, 0, parent] = piece.reshape(half // share, share, columns)
                else:
                    out_ref[0, parent] = piece

    def early(i):
        return jnp.minimum(i, 7)

    def late(i):
        return jnp.maximum(i - 8, 0)

    if split:
        out_shape = (parts, 2, parents, share, columns)
        out_spec = pl.BlockSpec(
            (parts // 2, 1, parents, share, columns),
            lambda i: (late(i) % 2, late(i) // 2, 0, 0, 0),
        )
    else:
        out_shape = (2, parents, directions, columns)
        out_spec = pl.BlockSpec(
            (1, parents, half, columns), lambda i: (late(i) // 2, 0, late(i) % 2, 0)
        )
    out = pl.pallas_call(
        body,
        grid=(12,),
        in_specs=[
            pl.BlockSpec((2, parents, 1, unknowns, columns), lambda i: (0, 0, early(i), 0, 0)),
            pl.BlockSpec((parents, 1, 2, leaf_dirs, unknowns), lambda i: (0, early(i), 0, 0, 0)),
            pl.BlockSpec((directions, leaf_dirs), lambda i: (0, 0)),
            pl.BlockSpec((directions, 8), lambda i: (0, 0)),
            pl.BlockSpec((directions, 8), lambda i: (0, 0)),
        ],
        out_specs=out_spec,
        out_shape=jax.ShapeDtypeStruct(out_shape, jnp.bfloat16),
        scratch_shapes=[
            pltpu.VMEM((8 * width, parents * columns), jnp.bfloat16),
            pltpu.VMEM((8, 2 * directions, width), jnp.bfloat16),
        ],
        compiler_params=pltpu.CompilerParams(vmem_limit_bytes=VMEM_BYTES),
        name="upward",
    )(currents, radiate, interp, cosine.T, sine.T)
    if not split:
        out = out.reshape(2, parents, parts, share, columns)
        out = jnp.transpose(out, (2, 0, 1, 3, 4))
    return out


def near_products(lower, currents, upper, near_tiles, near_index, near_count, first):
    _, boxes, unknowns, columns = currents.shape
    reach = boxes // 2
    slots = near_tiles.shape[1]

    def body(index_ref, count_ref, low_ref, cur_ref, up_ref, tile_ref, out_ref, window, acc, sems):
        box = pl.program_id(0)

        @pl.when(box == 0)
        def _():
            copies = []
            for part in range(2):
                rows = pl.ds(part * unknowns, unknowns)
                for order, (ref, start, size) in enumerate(
                    ((low_ref, 0, reach), (cur_ref, reach, boxes), (up_ref, reach + boxes, reach))
                ):
                    copies.append(
                        pltpu.make_async_copy(
                            ref.at[part],
                            window.at[pl.ds(start, size), rows],
                            sems.at[3 * part + order],
                        )
                    )
            for copy in copies:
                copy.start()
            for copy in copies:
                copy.wait()

        def product(slot):
            mat = complex_matrix(tile_ref[0, slot, 0], tile_ref[0, slot, 1])
            return dot(mat, window[index_ref[box * slots + slot]])

        acc[...] = product(0) + product(1)

        def add(slot, carry):
            acc[...] += product(slot)
            return carry

        lax.fori_loop(2, count_ref[box], add, 0)
        total = acc[...].astype(jnp.bfloat16)
        out_ref[0, 0] = total[:unknowns]
        out_ref[1, 0] = total[unknowns:]

    local_index = jnp.clip(near_index - first, 0, 2 * boxes - 1).reshape(-1)
    flops = boxes * slots * 8 * unknowns * unknowns * columns
    return pl.pallas_call(
        body,
        grid_spec=pltpu.PrefetchScalarGridSpec(
            num_scalar_prefetch=2,
            grid=(boxes,),
            in_specs=[
                pl.BlockSpec(memory_space=pl.ANY),
                pl.BlockSpec(memory_space=pl.ANY),
                pl.BlockSpec(memory_space=pl.ANY),
                pl.BlockSpec(
                    (1, slots, 2, unknowns, unknowns), lambda b, index, count: (b, 0, 0, 0, 0)
                ),
            ],
            out_specs=pl.BlockSpec(
                (2, 1, unknowns, columns), lambda b, index, count: (0, b, 0, 0)
            ),
            scratch_shapes=[
                pltpu.VMEM((2 * boxes, 2 * unknowns, columns), jnp.bfloat16),
                pltpu.VMEM((2 * unknowns, columns), jnp.float32),
                pltpu.SemaphoreType.DMA((6,)),
            ],
        ),
        out_shape=jax.ShapeDtypeStruct(currents.shape, jnp.bfloat16),
        compiler_params=pltpu.CompilerParams(vmem_limit_bytes=VMEM_BYTES),
        cost_estimate=pl.CostEstimate(
            flops=flops,
            bytes_accessed=2 * near_tiles.size + 8 * currents.size,
            transcendentals=0,
        ),
        name="near_products",
    )(local_index, near_count, lower, currents, upper, near_tiles)


def translation_matrix(far_index, far_count, trans_index, translators):
    parent_total, slot_count = far_index.shape
    operators, _, share = translators.shape
    slot_ids = jnp.arange(slot_count, dtype=jnp.int32)
    live = slot_ids[None, :] < far_count[:, None]
    chosen = jnp.where(live, trans_index, -1).reshape(-1)
    pick = (chosen[:, None] == jnp.arange(operators, dtype=jnp.int32)[None, :]).astype(jnp.bfloat16)
    table = translators.reshape(operators, 2 * share)
    factor = dot(pick, table.astype(jnp.bfloat16)).astype(jnp.bfloat16)
    factor = factor.reshape(parent_total, slot_count, 2 * share)
    parent_ids = jnp.arange(parent_total, dtype=jnp.int32)
    selector = (far_index[:, :, None] == parent_ids[None, None, :]).astype(jnp.bfloat16)
    matrix = jnp.einsum("psx,psq->xpq", factor, selector, preferred_element_type=jnp.float32)
    return matrix.astype(jnp.bfloat16)


def wire_matrix(matrix, parts):
    share = matrix.shape[0] // 2
    total = matrix.shape[1]
    each = total // parts
    place = jnp.arange(2 * total, dtype=jnp.int32)
    parent = place // (2 * each) * each + place % each
    same = parent[:, None] == jnp.arange(total, dtype=jnp.int32)[None, :]
    part = place // each % 2
    spread = jnp.stack([same & (part == c)[:, None] for c in range(2)]).astype(jnp.bfloat16)
    gather = jnp.transpose(spread, (0, 2, 1))

    def body(real_ref, imag_ref, spread_ref, gather_ref, out_ref):
        real = real_ref[0]
        imag = imag_ref[0]
        top = dot(real, gather_ref[0]) - dot(imag, gather_ref[1])
        bottom = dot(imag, gather_ref[0]) + dot(real, gather_ref[1])
        result = dot(spread_ref[0], top.astype(jnp.bfloat16))
        result = result + dot(spread_ref[1], bottom.astype(jnp.bfloat16))
        out_ref[0] = result.astype(jnp.bfloat16)

    return pl.pallas_call(
        body,
        grid=(share,),
        in_specs=[
            pl.BlockSpec((1, total, total), lambda j: (j, 0, 0)),
            pl.BlockSpec((1, total, total), lambda j: (share + j, 0, 0)),
            pl.BlockSpec((2, 2 * total, total), lambda j: (0, 0, 0)),
            pl.BlockSpec((2, total, 2 * total), lambda j: (0, 0, 0)),
        ],
        out_specs=pl.BlockSpec((1, 2 * total, 2 * total), lambda j: (j, 0, 0)),
        out_shape=jax.ShapeDtypeStruct((share, 2 * total, 2 * total), jnp.bfloat16),
        compiler_params=pltpu.CompilerParams(vmem_limit_bytes=VMEM_BYTES),
        cost_estimate=pl.CostEstimate(
            flops=16 * share * total**3, bytes_accessed=12 * share * total**2, transcendentals=0
        ),
        name="wire_matrix",
    )(matrix, matrix, spread, gather)


def translate(patterns, matrix):
    parts, _, parents, share, columns = patterns.shape
    rows = parts * 2 * parents
    half = columns // 2

    def body(in_ref, mat_ref, out_ref, wide, result):
        wide[...] = in_ref[...].astype(jnp.float32)

        for j in range(share):
            source = wide[pl.ds(j, rows, stride=share), :].astype(jnp.bfloat16)
            result[pl.ds(j, rows, stride=share), :] = dot(mat_ref[j], source)
        out_ref[...] = result[...].astype(jnp.bfloat16)

    out = pl.pallas_call(
        body,
        grid=(columns // half,),
        in_specs=[
            pl.BlockSpec((rows * share, half), lambda i: (0, i)),
            pl.BlockSpec((share, rows, rows), lambda i: (0, 0, 0)),
        ],
        out_specs=pl.BlockSpec((rows * share, half), lambda i: (0, i)),
        out_shape=jax.ShapeDtypeStruct((rows * share, columns), jnp.bfloat16),
        scratch_shapes=[
            pltpu.VMEM((rows * share, half), jnp.float32),
            pltpu.VMEM((rows * share, half), jnp.float32),
        ],
        compiler_params=pltpu.CompilerParams(vmem_limit_bytes=VMEM_BYTES),
        name="translate",
    )(patterns.reshape(rows * share, columns), matrix)
    return out.reshape(patterns.shape)


def downward(incoming, near, receive, interp_t, cosine, sine):
    parts, _, parents, share, columns = incoming.shape
    _, boxes, unknowns, _ = near.shape
    leaf_dirs, directions = interp_t.shape
    split = share % 16 == 0
    near = near.reshape(2, parents, 8, unknowns, columns)
    receive = receive.reshape(parents, 8, 2, unknowns, leaf_dirs)
    if not split:
        incoming = jnp.transpose(incoming, (1, 2, 0, 3, 4)).reshape(2, parents, directions, columns)

    def body(in_ref, near_ref, rec_ref, interp_ref, cos_ref, sin_ref, out_ref, source):
        @pl.when(pl.program_id(0) == 0)
        def _():
            for part in range(2):
                for parent in range(parents):
                    if split:
                        piece = in_ref[:, part, parent].reshape(directions, columns)
                    else:
                        piece = in_ref[part, parent]
                    source[
                        part * directions : (part + 1) * directions,
                        parent * columns : (parent + 1) * columns,
                    ] = piece

        wide = interp_ref[...].astype(jnp.float32)
        real = (wide * cos_ref[0]).astype(jnp.bfloat16)
        imag = (wide * sin_ref[0]).astype(jnp.bfloat16)
        arriving = dot(complex_matrix(real, -imag), source[...]).astype(jnp.bfloat16)
        for parent in range(parents):
            mat = complex_matrix(rec_ref[parent, 0, 0], rec_ref[parent, 0, 1])
            far = dot(mat, arriving[:, parent * columns : (parent + 1) * columns])
            for part in range(2):
                total = near_ref[part, parent, 0].astype(jnp.float32)
                total = total + far[part * unknowns : (part + 1) * unknowns]
                out_ref[part, parent, 0] = total.astype(jnp.bfloat16)

    whole = (0,) * incoming.ndim
    out = pl.pallas_call(
        body,
        grid=(8,),
        in_specs=[
            pl.BlockSpec(incoming.shape, lambda i: whole),
            pl.BlockSpec((2, parents, 1, unknowns, columns), lambda i: (0, 0, i, 0, 0)),
            pl.BlockSpec((parents, 1, 2, unknowns, leaf_dirs), lambda i: (0, i, 0, 0, 0)),
            pl.BlockSpec((leaf_dirs, directions), lambda i: (0, 0)),
            pl.BlockSpec((1, 1, directions), lambda i: (i, 0, 0)),
            pl.BlockSpec((1, 1, directions), lambda i: (i, 0, 0)),
        ],
        out_specs=pl.BlockSpec((2, parents, 1, unknowns, columns), lambda i: (0, 0, i, 0, 0)),
        out_shape=jax.ShapeDtypeStruct(near.shape, jnp.bfloat16),
        scratch_shapes=[pltpu.VMEM((2 * directions, parents * columns), jnp.bfloat16)],
        compiler_params=pltpu.CompilerParams(vmem_limit_bytes=VMEM_BYTES),
        name="downward",
    )(incoming, near, receive, interp_t, cosine[:, None, :], sine[:, None, :])
    return out.reshape(2, boxes, unknowns, columns)


def local(
    currents,
    near_tiles,
    near_index,
    near_count,
    radiate,
    receive,
    interp,
    shift_angle,
    far_index,
    far_count,
    trans_index,
    translators,
):
    boxes = currents.shape[1]
    reach = boxes // 2
    parts = lax.axis_size(AXES)
    lower = passed_along(currents[:, boxes - reach :], AXES, 1)
    upper = passed_along(currents[:, :reach], AXES, -1)
    cosine = jnp.cos(shift_angle)
    sine = jnp.sin(shift_angle)
    parent = upward(currents, radiate, interp, cosine, sine, parts)
    parent, near_count, far_index, trans_index, translators = lax.optimization_barrier(
        (parent, near_count, far_index, trans_index, translators)
    )
    by_direction = lax.all_to_all(parent, AXES, split_axis=0, concat_axis=0, tiled=True)
    matrix = wire_matrix(
        translation_matrix(far_index, far_count, trans_index, translators), parts
    )
    first = lax.axis_index(AXES) * boxes - reach
    near = near_products(lower, currents, upper, near_tiles, near_index, near_count, first)
    translated = translate(by_direction, matrix)
    incoming = lax.all_to_all(translated, AXES, split_axis=0, concat_axis=0, tiled=True)
    return downward(incoming, near, receive, interp.T, cosine, sine)


def solution(mesh):
    placed = (
        P(None, ("box", "dir"), None, None),
        P(("box", "dir"), None, None, None, None),
        P(("box", "dir"), None),
        P(("box", "dir")),
        P(("box", "dir"), None, None, None),
        P(("box", "dir"), None, None, None),
        P(),
        P(),
        P(),
        P(),
        P(),
        P(None, None, ("box", "dir")),
    )
    return jax.shard_map(
        local,
        mesh=mesh,
        in_specs=placed,
        out_specs=P(None, ("box", "dir"), None, None),
        check_vma=False,
    )
```

```python
import jax
import jax.numpy as jnp
from jax import lax
from jax.experimental import pallas as pl
from jax.experimental.pallas import tpu as pltpu
from jax.sharding import PartitionSpec as P

AXES = ("box", "dir")
VMEM_BYTES = 48 * 1024 * 1024


def passed_along(value, axis, by):
    peers = lax.axis_size(axis)
    pairs = [(i, i + by) for i in range(peers) if 0 <= i + by < peers]
    return lax.ppermute(value, axis, pairs)


def complex_matrix(real, imag):
    top = jnp.concatenate([real, -imag], axis=1)
    bottom = jnp.concatenate([imag, real], axis=1)
    return jnp.concatenate([top, bottom], axis=0)


def dot(left, right):
    return jnp.dot(left, right, preferred_element_type=jnp.float32)


def upward(currents, radiate, interp, cosine, sine, parts):
    _, boxes, unknowns, columns = currents.shape
    parents = boxes // 8
    directions, leaf_dirs = interp.shape
    share = directions // parts
    split = share % 16 == 0
    width = 2 * leaf_dirs
    currents = currents.reshape(2, parents, 8, unknowns, columns)
    radiate = radiate.reshape(parents, 8, 2, leaf_dirs, unknowns)

    def body(cur_ref, rad_ref, interp_ref, cos_ref, sin_ref, out_ref, leaf_ref, shift_ref):
        step = pl.program_id(0)

        @pl.when(step == 0)
        def _():
            wide = interp_ref[...].astype(jnp.float32)
            for c in range(8):
                real = (wide * cos_ref[:, c : c + 1]).astype(jnp.bfloat16)
                imag = (wide * sin_ref[:, c : c + 1]).astype(jnp.bfloat16)
                shift_ref[:, c * width : (c + 1) * width] = complex_matrix(real, imag)

        @pl.when(step < 8)
        def _():
            rows = pl.ds(pl.multiple_of(step * width, width), width)
            for parent in range(parents):
                mat = complex_matrix(rad_ref[parent, 0, 0], rad_ref[parent, 0, 1])
                vec = jnp.concatenate([cur_ref[0, parent, 0], cur_ref[1, parent, 0]], axis=0)
                leaf = dot(mat, vec).astype(jnp.bfloat16)
                leaf_ref[parent, rows, :] = leaf
        @pl.when(step >= 8)
        def _():
            source = leaf_ref[step - 8]
            for part in range(2):
                rows = slice(part * directions, (part + 1) * directions)
                piece = dot(shift_ref[rows, :], source).astype(jnp.bfloat16)
                if split:
                    out_ref[:, part, 0] = piece.reshape(parts, share, columns)
                else:
                    out_ref[part, 0] = piece

    def early(i):
        return jnp.minimum(i, 7)

    def late(i):
        return jnp.maximum(i - 8, 0)

    if split:
        out_shape = (parts, 2, parents, share, columns)
        out_spec = pl.BlockSpec(
            (parts, 2, 1, share, columns), lambda i: (0, 0, late(i), 0, 0)
        )
    else:
        out_shape = (2, parents, directions, columns)
        out_spec = pl.BlockSpec(
            (2, 1, directions, columns), lambda i: (0, late(i), 0, 0)
        )
    out = pl.pallas_call(
        body,
        grid=(8 + parents,),
        in_specs=[
            pl.BlockSpec((2, parents, 1, unknowns, columns), lambda i: (0, 0, early(i), 0, 0)),
            pl.BlockSpec((parents, 1, 2, leaf_dirs, unknowns), lambda i: (0, early(i), 0, 0, 0)),
            pl.BlockSpec((directions, leaf_dirs), lambda i: (0, 0)),
            pl.BlockSpec((directions, 8), lambda i: (0, 0)),
            pl.BlockSpec((directions, 8), lambda i: (0, 0)),
        ],
        out_specs=out_spec,
        out_shape=jax.ShapeDtypeStruct(out_shape, jnp.bfloat16),
        scratch_shapes=[
            pltpu.VMEM((parents, 8 * width, columns), jnp.bfloat16),
            pltpu.VMEM((2 * directions, 8 * width), jnp.bfloat16),
        ],
        compiler_params=pltpu.CompilerParams(vmem_limit_bytes=VMEM_BYTES),
        name="upward",
    )(currents, radiate, interp, cosine.T, sine.T)
    if not split:
        out = out.reshape(2, parents, parts, share, columns)
        out = jnp.transpose(out, (2, 0, 1, 3, 4))
    return out


def near_products(lower, currents, upper, near_tiles, near_index, near_count, first):
    _, boxes, unknowns, columns = currents.shape
    reach = boxes // 2
    slots = near_tiles.shape[1]

    def body(index_ref, count_ref, low_ref, cur_ref, up_ref, tile_ref, out_ref, window, acc, sems):
        box = pl.program_id(0)

        @pl.when(box == 0)
        def _():
            copies = []
            for part in range(2):
                rows = pl.ds(part * unknowns, unknowns)
                for order, (ref, start, size) in enumerate(
                    ((low_ref, 0, reach), (cur_ref, reach, boxes), (up_ref, reach + boxes, reach))
                ):
                    copies.append(
                        pltpu.make_async_copy(
                            ref.at[part],
                            window.at[pl.ds(start, size), rows],
                            sems.at[3 * part + order],
                        )
                    )
            for copy in copies:
                copy.start()
            for copy in copies:
                copy.wait()

        def product(slot):
            mat = complex_matrix(tile_ref[0, slot, 0], tile_ref[0, slot, 1])
            return dot(mat, window[index_ref[box * slots + slot]])

        acc[...] = product(0) + product(1)

        def add(slot, carry):
            acc[...] += product(slot)
            return carry

        lax.fori_loop(2, count_ref[box], add, 0)
        total = acc[...].astype(jnp.bfloat16)
        out_ref[0, 0] = total[:unknowns]
        out_ref[1, 0] = total[unknowns:]

    local_index = jnp.clip(near_index - first, 0, 2 * boxes - 1).reshape(-1)
    flops = boxes * slots * 8 * unknowns * unknowns * columns
    return pl.pallas_call(
        body,
        grid_spec=pltpu.PrefetchScalarGridSpec(
            num_scalar_prefetch=2,
            grid=(boxes,),
            in_specs=[
                pl.BlockSpec(memory_space=pl.ANY),
                pl.BlockSpec(memory_space=pl.ANY),
                pl.BlockSpec(memory_space=pl.ANY),
                pl.BlockSpec(
                    (1, slots, 2, unknowns, unknowns), lambda b, index, count: (b, 0, 0, 0, 0)
                ),
            ],
            out_specs=pl.BlockSpec(
                (2, 1, unknowns, columns), lambda b, index, count: (0, b, 0, 0)
            ),
            scratch_shapes=[
                pltpu.VMEM((2 * boxes, 2 * unknowns, columns), jnp.bfloat16),
                pltpu.VMEM((2 * unknowns, columns), jnp.float32),
                pltpu.SemaphoreType.DMA((6,)),
            ],
        ),
        out_shape=jax.ShapeDtypeStruct(currents.shape, jnp.bfloat16),
        compiler_params=pltpu.CompilerParams(vmem_limit_bytes=VMEM_BYTES),
        cost_estimate=pl.CostEstimate(
            flops=flops,
            bytes_accessed=2 * near_tiles.size + 8 * currents.size,
            transcendentals=0,
        ),
        name="near_products",
    )(local_index, near_count, lower, currents, upper, near_tiles)


def translation_matrix(far_index, far_count, trans_index, translators):
    parent_total, slot_count = far_index.shape
    operators, _, share = translators.shape
    slot_ids = jnp.arange(slot_count, dtype=jnp.int32)
    live = slot_ids[None, :] < far_count[:, None]
    chosen = jnp.where(live, trans_index, -1).reshape(-1)
    pick = (chosen[:, None] == jnp.arange(operators, dtype=jnp.int32)[None, :]).astype(jnp.bfloat16)
    table = translators.reshape(operators, 2 * share)
    factor = dot(pick, table.astype(jnp.bfloat16)).astype(jnp.bfloat16)
    factor = factor.reshape(parent_total, slot_count, 2 * share)
    parent_ids = jnp.arange(parent_total, dtype=jnp.int32)
    selector = (far_index[:, :, None] == parent_ids[None, None, :]).astype(jnp.bfloat16)
    matrix = jnp.einsum("psx,psq->xpq", factor, selector, preferred_element_type=jnp.float32)
    return matrix.astype(jnp.bfloat16)


def wire_matrix(matrix, parts):
    share = matrix.shape[0] // 2
    total = matrix.shape[1]
    each = total // parts
    place = jnp.arange(2 * total, dtype=jnp.int32)
    parent = place // (2 * each) * each + place % each
    same = parent[:, None] == jnp.arange(total, dtype=jnp.int32)[None, :]
    part = place // each % 2
    spread = jnp.stack([same & (part == c)[:, None] for c in range(2)]).astype(jnp.bfloat16)
    gather = jnp.transpose(spread, (0, 2, 1))

    def body(real_ref, imag_ref, spread_ref, gather_ref, out_ref):
        real = real_ref[0]
        imag = imag_ref[0]
        top = dot(real, gather_ref[0]) - dot(imag, gather_ref[1])
        bottom = dot(imag, gather_ref[0]) + dot(real, gather_ref[1])
        result = dot(spread_ref[0], top.astype(jnp.bfloat16))
        result = result + dot(spread_ref[1], bottom.astype(jnp.bfloat16))
        out_ref[0] = result.astype(jnp.bfloat16)

    return pl.pallas_call(
        body,
        grid=(share,),
        in_specs=[
            pl.BlockSpec((1, total, total), lambda j: (j, 0, 0)),
            pl.BlockSpec((1, total, total), lambda j: (share + j, 0, 0)),
            pl.BlockSpec((2, 2 * total, total), lambda j: (0, 0, 0)),
            pl.BlockSpec((2, total, 2 * total), lambda j: (0, 0, 0)),
        ],
        out_specs=pl.BlockSpec((1, 2 * total, 2 * total), lambda j: (j, 0, 0)),
        out_shape=jax.ShapeDtypeStruct((share, 2 * total, 2 * total), jnp.bfloat16),
        compiler_params=pltpu.CompilerParams(vmem_limit_bytes=VMEM_BYTES),
        cost_estimate=pl.CostEstimate(
            flops=16 * share * total**3, bytes_accessed=12 * share * total**2, transcendentals=0
        ),
        name="wire_matrix",
    )(matrix, matrix, spread, gather)


def translate(patterns, matrix):
    parts, _, parents, share, columns = patterns.shape
    rows = parts * 2 * parents
    half = columns // 2

    def body(in_ref, mat_ref, out_ref, wide, result):
        wide[...] = in_ref[...].astype(jnp.float32)

        for j in range(share):
            source = wide[pl.ds(j, rows, stride=share), :].astype(jnp.bfloat16)
            result[pl.ds(j, rows, stride=share), :] = dot(mat_ref[j], source)
        out_ref[...] = result[...].astype(jnp.bfloat16)

    out = pl.pallas_call(
        body,
        grid=(columns // half,),
        in_specs=[
            pl.BlockSpec((rows * share, half), lambda i: (0, i)),
            pl.BlockSpec((share, rows, rows), lambda i: (0, 0, 0)),
        ],
        out_specs=pl.BlockSpec((rows * share, half), lambda i: (0, i)),
        out_shape=jax.ShapeDtypeStruct((rows * share, columns), jnp.bfloat16),
        scratch_shapes=[
            pltpu.VMEM((rows * share, half), jnp.float32),
            pltpu.VMEM((rows * share, half), jnp.float32),
        ],
        compiler_params=pltpu.CompilerParams(vmem_limit_bytes=VMEM_BYTES),
        name="translate",
    )(patterns.reshape(rows * share, columns), matrix)
    return out.reshape(patterns.shape)


def downward(incoming, near, receive, interp_t, cosine, sine):
    parts, _, parents, share, columns = incoming.shape
    _, boxes, unknowns, _ = near.shape
    leaf_dirs, directions = interp_t.shape
    split = share % 16 == 0
    near = near.reshape(2, parents, 8, unknowns, columns)
    receive = receive.reshape(parents, 8, 2, unknowns, leaf_dirs)
    if not split:
        incoming = jnp.transpose(incoming, (1, 2, 0, 3, 4)).reshape(2, parents, directions, columns)

    width = 2 * leaf_dirs

    def body(in_ref, near_ref, rec_ref, interp_ref, cos_ref, sin_ref, out_ref, shift_ref, arriving):
        @pl.when(pl.program_id(0) == 0)
        def _():
            wide = interp_ref[...].astype(jnp.float32)
            for c in range(8):
                real = (wide * cos_ref[c : c + 1, :]).astype(jnp.bfloat16)
                imag = (wide * sin_ref[c : c + 1, :]).astype(jnp.bfloat16)
                shift_ref[c * width : (c + 1) * width, :] = complex_matrix(real, -imag)

        pieces = [
            in_ref[:, part, 0].reshape(directions, columns) if split else in_ref[part, 0]
            for part in range(2)
        ]
        source = jnp.concatenate(pieces, axis=0)
        arriving[...] = dot(shift_ref[...], source).astype(jnp.bfloat16)
        for c in range(8):
            mat = complex_matrix(rec_ref[0, c, 0], rec_ref[0, c, 1])
            far = dot(mat, arriving[c * width : (c + 1) * width, :])
            for part in range(2):
                total = near_ref[part, 0, c].astype(jnp.float32)
                total = total + far[part * unknowns : (part + 1) * unknowns]
                out_ref[part, 0, c] = total.astype(jnp.bfloat16)

    if split:
        in_spec = pl.BlockSpec((parts, 2, 1, share, columns), lambda p: (0, 0, p, 0, 0))
    else:
        in_spec = pl.BlockSpec((2, 1, directions, columns), lambda p: (0, p, 0, 0))
    out = pl.pallas_call(
        body,
        grid=(parents,),
        in_specs=[
            in_spec,
            pl.BlockSpec((2, 1, 8, unknowns, columns), lambda p: (0, p, 0, 0, 0)),
            pl.BlockSpec((1, 8, 2, unknowns, leaf_dirs), lambda p: (p, 0, 0, 0, 0)),
            pl.BlockSpec((leaf_dirs, directions), lambda p: (0, 0)),
            pl.BlockSpec((8, directions), lambda p: (0, 0)),
            pl.BlockSpec((8, directions), lambda p: (0, 0)),
        ],
        out_specs=pl.BlockSpec((2, 1, 8, unknowns, columns), lambda p: (0, p, 0, 0, 0)),
        out_shape=jax.ShapeDtypeStruct(near.shape, jnp.bfloat16),
        scratch_shapes=[
            pltpu.VMEM((8 * width, 2 * directions), jnp.bfloat16),
            pltpu.VMEM((8 * width, columns), jnp.bfloat16),
        ],
        compiler_params=pltpu.CompilerParams(vmem_limit_bytes=VMEM_BYTES),
        name="downward",
    )(incoming, near, receive, interp_t, cosine, sine)
    return out.reshape(2, boxes, unknowns, columns)


def local(
    currents,
    near_tiles,
    near_index,
    near_count,
    radiate,
    receive,
    interp,
    shift_angle,
    far_index,
    far_count,
    trans_index,
    translators,
):
    boxes = currents.shape[1]
    reach = boxes // 2
    parts = lax.axis_size(AXES)
    lower = passed_along(currents[:, boxes - reach :], AXES, 1)
    upper = passed_along(currents[:, :reach], AXES, -1)
    cosine = jnp.cos(shift_angle)
    sine = jnp.sin(shift_angle)
    parent = upward(currents, radiate, interp, cosine, sine, parts)
    parent, far_index, trans_index, translators = lax.optimization_barrier(
        (parent, far_index, trans_index, translators)
    )
    by_direction = lax.all_to_all(parent, AXES, split_axis=0, concat_axis=0, tiled=True)
    matrix = wire_matrix(
        translation_matrix(far_index, far_count, trans_index, translators), parts
    )
    first = lax.axis_index(AXES) * boxes - reach
    by_direction, lower, upper = lax.optimization_barrier((by_direction, lower, upper))
    translated = translate(by_direction, matrix)
    translated, near_count = lax.optimization_barrier((translated, near_count))
    near = near_products(lower, currents, upper, near_tiles, near_index, near_count, first)
    incoming = lax.all_to_all(translated, AXES, split_axis=0, concat_axis=0, tiled=True)
    return downward(incoming, near, receive, interp.T, cosine, sine)


def solution(mesh):
    placed = (
        P(None, ("box", "dir"), None, None),
        P(("box", "dir"), None, None, None, None),
        P(("box", "dir"), None),
        P(("box", "dir")),
        P(("box", "dir"), None, None, None),
        P(("box", "dir"), None, None, None),
        P(),
        P(),
        P(),
        P(),
        P(),
        P(None, None, ("box", "dir")),
    )
    return jax.shard_map(
        local,
        mesh=mesh,
        in_specs=placed,
        out_specs=P(None, ("box", "dir"), None, None),
        check_vma=False,
    )
```

```python
import jax
import jax.numpy as jnp
from jax import lax
from jax.experimental import pallas as pl
from jax.experimental.pallas import tpu as pltpu
from jax.sharding import PartitionSpec as P

AXES = ("box", "dir")
VMEM_BYTES = 48 * 1024 * 1024


def passed_along(value, axis, by):
    peers = lax.axis_size(axis)
    pairs = [(i, i + by) for i in range(peers) if 0 <= i + by < peers]
    return lax.ppermute(value, axis, pairs)


def complex_matrix(real, imag):
    top = jnp.concatenate([real, -imag], axis=1)
    bottom = jnp.concatenate([imag, real], axis=1)
    return jnp.concatenate([top, bottom], axis=0)


def dot(left, right):
    return jnp.dot(left, right, preferred_element_type=jnp.float32)


def upward(currents, radiate, interp, cosine, sine, parts):
    _, boxes, unknowns, columns = currents.shape
    parents = boxes // 8
    directions, leaf_dirs = interp.shape
    share = directions // parts
    split = share % 16 == 0
    width = 2 * leaf_dirs
    currents = currents.reshape(2, parents, 8, unknowns, columns)
    radiate = radiate.reshape(parents, 8, 2, leaf_dirs, unknowns)

    def body(cur_ref, rad_ref, interp_ref, cos_ref, sin_ref, out_ref, leaf_ref, shift_ref):
        step = pl.program_id(0)

        @pl.when(step == 0)
        def _():
            wide = interp_ref[...].astype(jnp.float32)
            for c in range(8):
                real = (wide * cos_ref[:, c : c + 1]).astype(jnp.bfloat16)
                imag = (wide * sin_ref[:, c : c + 1]).astype(jnp.bfloat16)
                shift_ref[:, c * width : (c + 1) * width] = complex_matrix(real, imag)

        @pl.when(step < 8)
        def _():
            rows = pl.ds(pl.multiple_of(step * width, width), width)
            for parent in range(parents):
                mat = complex_matrix(rad_ref[parent, 0, 0], rad_ref[parent, 0, 1])
                vec = jnp.concatenate([cur_ref[0, parent, 0], cur_ref[1, parent, 0]], axis=0)
                leaf = dot(mat, vec).astype(jnp.bfloat16)
                leaf_ref[parent, rows, :] = leaf
        @pl.when(step >= 8)
        def _():
            source = leaf_ref[step - 8]
            for part in range(2):
                rows = slice(part * directions, (part + 1) * directions)
                piece = dot(shift_ref[rows, :], source).astype(jnp.bfloat16)
                if split:
                    out_ref[:, part, 0] = piece.reshape(parts, share, columns)
                else:
                    out_ref[part, 0] = piece

    def early(i):
        return jnp.minimum(i, 7)

    def late(i):
        return jnp.maximum(i - 8, 0)

    if split:
        out_shape = (parts, 2, parents, share, columns)
        out_spec = pl.BlockSpec(
            (parts, 2, 1, share, columns), lambda i: (0, 0, late(i), 0, 0)
        )
    else:
        out_shape = (2, parents, directions, columns)
        out_spec = pl.BlockSpec(
            (2, 1, directions, columns), lambda i: (0, late(i), 0, 0)
        )
    out = pl.pallas_call(
        body,
        grid=(8 + parents,),
        in_specs=[
            pl.BlockSpec((2, parents, 1, unknowns, columns), lambda i: (0, 0, early(i), 0, 0)),
            pl.BlockSpec((parents, 1, 2, leaf_dirs, unknowns), lambda i: (0, early(i), 0, 0, 0)),
            pl.BlockSpec((directions, leaf_dirs), lambda i: (0, 0)),
            pl.BlockSpec((directions, 8), lambda i: (0, 0)),
            pl.BlockSpec((directions, 8), lambda i: (0, 0)),
        ],
        out_specs=out_spec,
        out_shape=jax.ShapeDtypeStruct(out_shape, jnp.bfloat16),
        scratch_shapes=[
            pltpu.VMEM((parents, 8 * width, columns), jnp.bfloat16),
            pltpu.VMEM((2 * directions, 8 * width), jnp.bfloat16),
        ],
        compiler_params=pltpu.CompilerParams(vmem_limit_bytes=VMEM_BYTES),
        cost_estimate=pl.CostEstimate(
            flops=8 * boxes * leaf_dirs * columns * (unknowns + directions),
            bytes_accessed=2 * (currents.size + radiate.size + 2 * parents * directions * columns),
            transcendentals=0,
        ),
        name="upward",
    )(currents, radiate, interp, cosine.T, sine.T)
    if not split:
        out = out.reshape(2, parents, parts, share, columns)
        out = jnp.transpose(out, (2, 0, 1, 3, 4))
    return out


def near_products(lower, currents, upper, near_tiles, near_index, near_count, first):
    _, boxes, unknowns, columns = currents.shape
    reach = boxes // 2
    slots = near_tiles.shape[1]

    def body(index_ref, count_ref, low_ref, cur_ref, up_ref, tile_ref, out_ref, window, acc, sems):
        box = pl.program_id(0)

        @pl.when(box == 0)
        def _():
            copies = []
            for part in range(2):
                rows = pl.ds(part * unknowns, unknowns)
                for order, (ref, start, size) in enumerate(
                    ((low_ref, 0, reach), (cur_ref, reach, boxes), (up_ref, reach + boxes, reach))
                ):
                    copies.append(
                        pltpu.make_async_copy(
                            ref.at[part],
                            window.at[pl.ds(start, size), rows],
                            sems.at[3 * part + order],
                        )
                    )
            for copy in copies:
                copy.start()
            for copy in copies:
                copy.wait()

        def product(slot):
            mat = complex_matrix(tile_ref[0, slot, 0], tile_ref[0, slot, 1])
            return dot(mat, window[index_ref[box * slots + slot]])

        acc[...] = product(0) + product(1)

        def add(slot, carry):
            acc[...] += product(slot)
            return carry

        lax.fori_loop(2, count_ref[box], add, 0)
        total = acc[...].astype(jnp.bfloat16)
        out_ref[0, 0] = total[:unknowns]
        out_ref[1, 0] = total[unknowns:]

    local_index = jnp.clip(near_index - first, 0, 2 * boxes - 1).reshape(-1)
    flops = boxes * slots * 8 * unknowns * unknowns * columns
    return pl.pallas_call(
        body,
        grid_spec=pltpu.PrefetchScalarGridSpec(
            num_scalar_prefetch=2,
            grid=(boxes,),
            in_specs=[
                pl.BlockSpec(memory_space=pl.ANY),
                pl.BlockSpec(memory_space=pl.ANY),
                pl.BlockSpec(memory_space=pl.ANY),
                pl.BlockSpec(
                    (1, slots, 2, unknowns, unknowns), lambda b, index, count: (b, 0, 0, 0, 0)
                ),
            ],
            out_specs=pl.BlockSpec(
                (2, 1, unknowns, columns), lambda b, index, count: (0, b, 0, 0)
            ),
            scratch_shapes=[
                pltpu.VMEM((2 * boxes, 2 * unknowns, columns), jnp.bfloat16),
                pltpu.VMEM((2 * unknowns, columns), jnp.float32),
                pltpu.SemaphoreType.DMA((6,)),
            ],
        ),
        out_shape=jax.ShapeDtypeStruct(currents.shape, jnp.bfloat16),
        compiler_params=pltpu.CompilerParams(vmem_limit_bytes=VMEM_BYTES),
        cost_estimate=pl.CostEstimate(
            flops=flops,
            bytes_accessed=2 * near_tiles.size + 8 * currents.size,
            transcendentals=0,
        ),
        name="near_products",
    )(local_index, near_count, lower, currents, upper, near_tiles)


def translation_matrix(far_index, far_count, trans_index, translators):
    parent_total, slot_count = far_index.shape
    operators, _, share = translators.shape
    slot_ids = jnp.arange(slot_count, dtype=jnp.int32)
    live = slot_ids[None, :] < far_count[:, None]
    chosen = jnp.where(live, trans_index, -1).reshape(-1)
    pick = (chosen[:, None] == jnp.arange(operators, dtype=jnp.int32)[None, :]).astype(jnp.bfloat16)
    table = translators.reshape(operators, 2 * share)
    factor = dot(pick, table.astype(jnp.bfloat16)).astype(jnp.bfloat16)
    factor = factor.reshape(parent_total, slot_count, 2 * share)
    parent_ids = jnp.arange(parent_total, dtype=jnp.int32)
    selector = (far_index[:, :, None] == parent_ids[None, None, :]).astype(jnp.bfloat16)
    matrix = jnp.einsum("psx,psq->xpq", factor, selector, preferred_element_type=jnp.float32)
    return matrix.astype(jnp.bfloat16)


def wire_matrix(matrix, parts):
    share = matrix.shape[0] // 2
    total = matrix.shape[1]
    each = total // parts
    place = jnp.arange(2 * total, dtype=jnp.int32)
    parent = place // (2 * each) * each + place % each
    same = parent[:, None] == jnp.arange(total, dtype=jnp.int32)[None, :]
    part = place // each % 2
    spread = jnp.stack([same & (part == c)[:, None] for c in range(2)]).astype(jnp.bfloat16)
    gather = jnp.transpose(spread, (0, 2, 1))

    def body(real_ref, imag_ref, spread_ref, gather_ref, out_ref):
        real = real_ref[0]
        imag = imag_ref[0]
        top = dot(real, gather_ref[0]) - dot(imag, gather_ref[1])
        bottom = dot(imag, gather_ref[0]) + dot(real, gather_ref[1])
        result = dot(spread_ref[0], top.astype(jnp.bfloat16))
        result = result + dot(spread_ref[1], bottom.astype(jnp.bfloat16))
        out_ref[0] = result.astype(jnp.bfloat16)

    return pl.pallas_call(
        body,
        grid=(share,),
        in_specs=[
            pl.BlockSpec((1, total, total), lambda j: (j, 0, 0)),
            pl.BlockSpec((1, total, total), lambda j: (share + j, 0, 0)),
            pl.BlockSpec((2, 2 * total, total), lambda j: (0, 0, 0)),
            pl.BlockSpec((2, total, 2 * total), lambda j: (0, 0, 0)),
        ],
        out_specs=pl.BlockSpec((1, 2 * total, 2 * total), lambda j: (j, 0, 0)),
        out_shape=jax.ShapeDtypeStruct((share, 2 * total, 2 * total), jnp.bfloat16),
        compiler_params=pltpu.CompilerParams(vmem_limit_bytes=VMEM_BYTES),
        cost_estimate=pl.CostEstimate(
            flops=16 * share * total**3, bytes_accessed=12 * share * total**2, transcendentals=0
        ),
        name="wire_matrix",
    )(matrix, matrix, spread, gather)


def translate(patterns, matrix):
    parts, _, parents, share, columns = patterns.shape
    rows = parts * 2 * parents
    half = columns // 2

    def body(in_ref, mat_ref, out_ref, wide, result):
        wide[...] = in_ref[...].astype(jnp.float32)

        for j in range(share):
            source = wide[pl.ds(j, rows, stride=share), :].astype(jnp.bfloat16)
            result[pl.ds(j, rows, stride=share), :] = dot(mat_ref[j], source)
        out_ref[...] = result[...].astype(jnp.bfloat16)

    out = pl.pallas_call(
        body,
        grid=(columns // half,),
        in_specs=[
            pl.BlockSpec((rows * share, half), lambda i: (0, i)),
            pl.BlockSpec((share, rows, rows), lambda i: (0, 0, 0)),
        ],
        out_specs=pl.BlockSpec((rows * share, half), lambda i: (0, i)),
        out_shape=jax.ShapeDtypeStruct((rows * share, columns), jnp.bfloat16),
        scratch_shapes=[
            pltpu.VMEM((rows * share, half), jnp.float32),
            pltpu.VMEM((rows * share, half), jnp.float32),
        ],
        compiler_params=pltpu.CompilerParams(vmem_limit_bytes=VMEM_BYTES),
        name="translate",
    )(patterns.reshape(rows * share, columns), matrix)
    return out.reshape(patterns.shape)


def downward(incoming, near, receive, interp_t, cosine, sine):
    parts, _, parents, share, columns = incoming.shape
    _, boxes, unknowns, _ = near.shape
    leaf_dirs, directions = interp_t.shape
    split = share % 16 == 0
    near = near.reshape(2, parents, 8, unknowns, columns)
    receive = receive.reshape(parents, 8, 2, unknowns, leaf_dirs)
    if not split:
        incoming = jnp.transpose(incoming, (1, 2, 0, 3, 4)).reshape(2, parents, directions, columns)

    width = 2 * leaf_dirs

    def body(in_ref, near_ref, rec_ref, interp_ref, cos_ref, sin_ref, out_ref, shift_ref, arriving):
        @pl.when(pl.program_id(0) == 0)
        def _():
            wide = interp_ref[...].astype(jnp.float32)
            for c in range(8):
                real = (wide * cos_ref[c : c + 1, :]).astype(jnp.bfloat16)
                imag = (wide * sin_ref[c : c + 1, :]).astype(jnp.bfloat16)
                shift_ref[c * width : (c + 1) * width, :] = complex_matrix(real, -imag)

        pieces = [
            in_ref[:, part, 0].reshape(directions, columns) if split else in_ref[part, 0]
            for part in range(2)
        ]
        source = jnp.concatenate(pieces, axis=0)
        arriving[...] = dot(shift_ref[...], source).astype(jnp.bfloat16)
        for c in range(8):
            mat = complex_matrix(rec_ref[0, c, 0], rec_ref[0, c, 1])
            far = dot(mat, arriving[c * width : (c + 1) * width, :])
            for part in range(2):
                total = near_ref[part, 0, c].astype(jnp.float32)
                total = total + far[part * unknowns : (part + 1) * unknowns]
                out_ref[part, 0, c] = total.astype(jnp.bfloat16)

    if split:
        in_spec = pl.BlockSpec((parts, 2, 1, share, columns), lambda p: (0, 0, p, 0, 0))
    else:
        in_spec = pl.BlockSpec((2, 1, directions, columns), lambda p: (0, p, 0, 0))
    out = pl.pallas_call(
        body,
        grid=(parents,),
        in_specs=[
            in_spec,
            pl.BlockSpec((2, 1, 8, unknowns, columns), lambda p: (0, p, 0, 0, 0)),
            pl.BlockSpec((1, 8, 2, unknowns, leaf_dirs), lambda p: (p, 0, 0, 0, 0)),
            pl.BlockSpec((leaf_dirs, directions), lambda p: (0, 0)),
            pl.BlockSpec((8, directions), lambda p: (0, 0)),
            pl.BlockSpec((8, directions), lambda p: (0, 0)),
        ],
        out_specs=pl.BlockSpec((2, 1, 8, unknowns, columns), lambda p: (0, p, 0, 0, 0)),
        out_shape=jax.ShapeDtypeStruct(near.shape, jnp.bfloat16),
        scratch_shapes=[
            pltpu.VMEM((8 * width, 2 * directions), jnp.bfloat16),
            pltpu.VMEM((8 * width, columns), jnp.bfloat16),
        ],
        compiler_params=pltpu.CompilerParams(vmem_limit_bytes=VMEM_BYTES),
        name="downward",
    )(incoming, near, receive, interp_t, cosine, sine)
    return out.reshape(2, boxes, unknowns, columns)


def local(
    currents,
    near_tiles,
    near_index,
    near_count,
    radiate,
    receive,
    interp,
    shift_angle,
    far_index,
    far_count,
    trans_index,
    translators,
):
    boxes = currents.shape[1]
    reach = boxes // 2
    parts = lax.axis_size(AXES)
    lower = passed_along(currents[:, boxes - reach :], AXES, 1)
    upper = passed_along(currents[:, :reach], AXES, -1)
    cosine = jnp.cos(shift_angle)
    sine = jnp.sin(shift_angle)
    parent = upward(currents, radiate, interp, cosine, sine, parts)
    parent, lower, upper, far_index, trans_index, translators = lax.optimization_barrier(
        (parent, lower, upper, far_index, trans_index, translators)
    )
    by_direction = lax.all_to_all(parent, AXES, split_axis=0, concat_axis=0, tiled=True)
    matrix = wire_matrix(
        translation_matrix(far_index, far_count, trans_index, translators), parts
    )
    first = lax.axis_index(AXES) * boxes - reach
    translated = translate(by_direction, matrix)
    translated, near_count = lax.optimization_barrier((translated, near_count))
    near = near_products(lower, currents, upper, near_tiles, near_index, near_count, first)
    incoming = lax.all_to_all(translated, AXES, split_axis=0, concat_axis=0, tiled=True)
    return downward(incoming, near, receive, interp.T, cosine, sine)


def solution(mesh):
    placed = (
        P(None, ("box", "dir"), None, None),
        P(("box", "dir"), None, None, None, None),
        P(("box", "dir"), None),
        P(("box", "dir")),
        P(("box", "dir"), None, None, None),
        P(("box", "dir"), None, None, None),
        P(),
        P(),
        P(),
        P(),
        P(),
        P(None, None, ("box", "dir")),
    )
    return jax.shard_map(
        local,
        mesh=mesh,
        in_specs=placed,
        out_specs=P(None, ("box", "dir"), None, None),
        check_vma=False,
    )
```

```python
import jax
import jax.numpy as jnp
from jax import lax
from jax.experimental import pallas as pl
from jax.experimental.pallas import tpu as pltpu
from jax.sharding import PartitionSpec as P

AXES = ("box", "dir")
VMEM_BYTES = 48 * 1024 * 1024


def passed_along(value, axis, by):
    peers = lax.axis_size(axis)
    pairs = [(i, i + by) for i in range(peers) if 0 <= i + by < peers]
    return lax.ppermute(value, axis, pairs)


def complex_matrix(real, imag):
    top = jnp.concatenate([real, -imag], axis=1)
    bottom = jnp.concatenate([imag, real], axis=1)
    return jnp.concatenate([top, bottom], axis=0)


def dot(left, right):
    return jnp.dot(left, right, preferred_element_type=jnp.float32)


def upward(currents, radiate, interp, cosine, sine, parts):
    _, boxes, unknowns, columns = currents.shape
    parents = boxes // 8
    directions, leaf_dirs = interp.shape
    share = directions // parts
    split = share % 16 == 0
    width = 2 * leaf_dirs
    currents = currents.reshape(2, parents, 8, unknowns, columns)
    radiate = radiate.reshape(parents, 8, 2, leaf_dirs, unknowns)

    def body(cur_ref, rad_ref, interp_ref, cos_ref, sin_ref, out_ref, leaf_ref, shift_ref):
        step = pl.program_id(0)

        @pl.when(step == 0)
        def _():
            wide = interp_ref[...].astype(jnp.float32)
            for c in range(8):
                real = (wide * cos_ref[:, c : c + 1]).astype(jnp.bfloat16)
                imag = (wide * sin_ref[:, c : c + 1]).astype(jnp.bfloat16)
                shift_ref[:, c * width : (c + 1) * width] = complex_matrix(real, imag)

        @pl.when(step < 8)
        def _():
            rows = pl.ds(pl.multiple_of(step * width, width), width)
            for parent in range(parents):
                mat = complex_matrix(rad_ref[parent, 0, 0], rad_ref[parent, 0, 1])
                vec = jnp.concatenate([cur_ref[0, parent, 0], cur_ref[1, parent, 0]], axis=0)
                leaf = dot(mat, vec).astype(jnp.bfloat16)
                leaf_ref[parent, rows, :] = leaf
        @pl.when(step >= 8)
        def _():
            source = leaf_ref[step - 8]
            for part in range(2):
                rows = slice(part * directions, (part + 1) * directions)
                piece = dot(shift_ref[rows, :], source).astype(jnp.bfloat16)
                if split:
                    out_ref[:, part, 0] = piece.reshape(parts, share, columns)
                else:
                    out_ref[part, 0] = piece

    def early(i):
        return jnp.minimum(i, 7)

    def late(i):
        return jnp.maximum(i - 8, 0)

    if split:
        out_shape = (parts, 2, parents, share, columns)
        out_spec = pl.BlockSpec(
            (parts, 2, 1, share, columns), lambda i: (0, 0, late(i), 0, 0)
        )
    else:
        out_shape = (2, parents, directions, columns)
        out_spec = pl.BlockSpec(
            (2, 1, directions, columns), lambda i: (0, late(i), 0, 0)
        )
    out = pl.pallas_call(
        body,
        grid=(8 + parents,),
        in_specs=[
            pl.BlockSpec((2, parents, 1, unknowns, columns), lambda i: (0, 0, early(i), 0, 0)),
            pl.BlockSpec((parents, 1, 2, leaf_dirs, unknowns), lambda i: (0, early(i), 0, 0, 0)),
            pl.BlockSpec((directions, leaf_dirs), lambda i: (0, 0)),
            pl.BlockSpec((directions, 8), lambda i: (0, 0)),
            pl.BlockSpec((directions, 8), lambda i: (0, 0)),
        ],
        out_specs=out_spec,
        out_shape=jax.ShapeDtypeStruct(out_shape, jnp.bfloat16),
        scratch_shapes=[
            pltpu.VMEM((parents, 8 * width, columns), jnp.bfloat16),
            pltpu.VMEM((2 * directions, 8 * width), jnp.bfloat16),
        ],
        compiler_params=pltpu.CompilerParams(vmem_limit_bytes=VMEM_BYTES),
        cost_estimate=pl.CostEstimate(
            flops=8 * boxes * leaf_dirs * columns * (unknowns + directions),
            bytes_accessed=2 * (currents.size + radiate.size + 2 * parents * directions * columns),
            transcendentals=0,
        ),
        name="upward",
    )(currents, radiate, interp, cosine.T, sine.T)
    if not split:
        out = out.reshape(2, parents, parts, share, columns)
        out = jnp.transpose(out, (2, 0, 1, 3, 4))
    return out


def near_products(lower, currents, upper, near_tiles, near_index, near_count, first):
    _, boxes, unknowns, columns = currents.shape
    reach = boxes // 2
    slots = near_tiles.shape[1]

    def body(
        index_ref,
        count_ref,
        low_real,
        low_imag,
        cur_ref,
        up_real,
        up_imag,
        tile_ref,
        out_ref,
        window,
        acc,
        sems,
    ):
        box = pl.program_id(0)

        @pl.when(box == 0)
        def _():
            copies = []
            for part in range(2):
                rows = pl.ds(part * unknowns, unknowns)
                for order, (ref, start, size) in enumerate(
                    (
                        ((low_real, low_imag)[part], 0, reach),
                        (cur_ref.at[part], reach, boxes),
                        ((up_real, up_imag)[part], reach + boxes, reach),
                    )
                ):
                    copies.append(
                        pltpu.make_async_copy(
                            ref,
                            window.at[pl.ds(start, size), rows],
                            sems.at[3 * part + order],
                        )
                    )
            for copy in copies:
                copy.start()
            for copy in copies:
                copy.wait()

        def product(slot):
            mat = complex_matrix(tile_ref[0, slot, 0], tile_ref[0, slot, 1])
            return dot(mat, window[index_ref[box * slots + slot]])

        acc[...] = product(0) + product(1)

        def add(slot, carry):
            acc[...] += product(slot)
            return carry

        lax.fori_loop(2, count_ref[box], add, 0)
        total = acc[...].astype(jnp.bfloat16)
        out_ref[0, 0] = total[:unknowns]
        out_ref[1, 0] = total[unknowns:]

    local_index = jnp.clip(near_index - first, 0, 2 * boxes - 1).reshape(-1)
    flops = boxes * slots * 8 * unknowns * unknowns * columns
    return pl.pallas_call(
        body,
        grid_spec=pltpu.PrefetchScalarGridSpec(
            num_scalar_prefetch=2,
            grid=(boxes,),
            in_specs=[
                pl.BlockSpec(memory_space=pl.ANY),
                pl.BlockSpec(memory_space=pl.ANY),
                pl.BlockSpec(memory_space=pl.ANY),
                pl.BlockSpec(memory_space=pl.ANY),
                pl.BlockSpec(memory_space=pl.ANY),
                pl.BlockSpec(
                    (1, slots, 2, unknowns, unknowns), lambda b, index, count: (b, 0, 0, 0, 0)
                ),
            ],
            out_specs=pl.BlockSpec(
                (2, 1, unknowns, columns), lambda b, index, count: (0, b, 0, 0)
            ),
            scratch_shapes=[
                pltpu.VMEM((2 * boxes, 2 * unknowns, columns), jnp.bfloat16),
                pltpu.VMEM((2 * unknowns, columns), jnp.float32),
                pltpu.SemaphoreType.DMA((6,)),
            ],
        ),
        out_shape=jax.ShapeDtypeStruct(currents.shape, jnp.bfloat16),
        compiler_params=pltpu.CompilerParams(vmem_limit_bytes=VMEM_BYTES),
        cost_estimate=pl.CostEstimate(
            flops=flops,
            bytes_accessed=2 * near_tiles.size + 8 * currents.size,
            transcendentals=0,
        ),
        name="near_products",
    )(local_index, near_count, *lower, currents, *upper, near_tiles)


def translation_matrix(far_index, far_count, trans_index, translators):
    parent_total, slot_count = far_index.shape
    operators, _, share = translators.shape
    slot_ids = jnp.arange(slot_count, dtype=jnp.int32)
    live = slot_ids[None, :] < far_count[:, None]
    chosen = jnp.where(live, trans_index, -1).reshape(-1)
    pick = (chosen[:, None] == jnp.arange(operators, dtype=jnp.int32)[None, :]).astype(jnp.bfloat16)
    table = translators.reshape(operators, 2 * share)
    factor = dot(pick, table.astype(jnp.bfloat16)).astype(jnp.bfloat16)
    factor = factor.reshape(parent_total, slot_count, 2 * share)
    parent_ids = jnp.arange(parent_total, dtype=jnp.int32)
    selector = (far_index[:, :, None] == parent_ids[None, None, :]).astype(jnp.bfloat16)
    matrix = jnp.einsum("psx,psq->xpq", factor, selector, preferred_element_type=jnp.float32)
    return matrix.astype(jnp.bfloat16)


def wire_matrix(matrix, parts):
    share = matrix.shape[0] // 2
    total = matrix.shape[1]
    each = total // parts
    place = jnp.arange(2 * total, dtype=jnp.int32)
    parent = place // (2 * each) * each + place % each
    same = parent[:, None] == jnp.arange(total, dtype=jnp.int32)[None, :]
    part = place // each % 2
    spread = jnp.stack([same & (part == c)[:, None] for c in range(2)]).astype(jnp.bfloat16)
    gather = jnp.transpose(spread, (0, 2, 1))

    def body(real_ref, imag_ref, spread_ref, gather_ref, out_ref):
        real = real_ref[0]
        imag = imag_ref[0]
        top = dot(real, gather_ref[0]) - dot(imag, gather_ref[1])
        bottom = dot(imag, gather_ref[0]) + dot(real, gather_ref[1])
        result = dot(spread_ref[0], top.astype(jnp.bfloat16))
        result = result + dot(spread_ref[1], bottom.astype(jnp.bfloat16))
        out_ref[0] = result.astype(jnp.bfloat16)

    return pl.pallas_call(
        body,
        grid=(share,),
        in_specs=[
            pl.BlockSpec((1, total, total), lambda j: (j, 0, 0)),
            pl.BlockSpec((1, total, total), lambda j: (share + j, 0, 0)),
            pl.BlockSpec((2, 2 * total, total), lambda j: (0, 0, 0)),
            pl.BlockSpec((2, total, 2 * total), lambda j: (0, 0, 0)),
        ],
        out_specs=pl.BlockSpec((1, 2 * total, 2 * total), lambda j: (j, 0, 0)),
        out_shape=jax.ShapeDtypeStruct((share, 2 * total, 2 * total), jnp.bfloat16),
        compiler_params=pltpu.CompilerParams(vmem_limit_bytes=VMEM_BYTES),
        cost_estimate=pl.CostEstimate(
            flops=16 * share * total**3, bytes_accessed=12 * share * total**2, transcendentals=0
        ),
        name="wire_matrix",
    )(matrix, matrix, spread, gather)


def translate(patterns, matrix):
    parts, _, parents, share, columns = patterns.shape
    rows = parts * 2 * parents
    half = columns // 2

    def body(in_ref, mat_ref, out_ref, wide, result):
        wide[...] = in_ref[...].astype(jnp.float32)

        for j in range(share):
            source = wide[pl.ds(j, rows, stride=share), :].astype(jnp.bfloat16)
            result[pl.ds(j, rows, stride=share), :] = dot(mat_ref[j], source)
        out_ref[...] = result[...].astype(jnp.bfloat16)

    out = pl.pallas_call(
        body,
        grid=(columns // half,),
        in_specs=[
            pl.BlockSpec((rows * share, half), lambda i: (0, i)),
            pl.BlockSpec((share, rows, rows), lambda i: (0, 0, 0)),
        ],
        out_specs=pl.BlockSpec((rows * share, half), lambda i: (0, i)),
        out_shape=jax.ShapeDtypeStruct((rows * share, columns), jnp.bfloat16),
        scratch_shapes=[
            pltpu.VMEM((rows * share, half), jnp.float32),
            pltpu.VMEM((rows * share, half), jnp.float32),
        ],
        compiler_params=pltpu.CompilerParams(vmem_limit_bytes=VMEM_BYTES),
        name="translate",
    )(patterns.reshape(rows * share, columns), matrix)
    return out.reshape(patterns.shape)


def downward(incoming, near, receive, interp_t, cosine, sine):
    parts, _, parents, share, columns = incoming.shape
    _, boxes, unknowns, _ = near.shape
    leaf_dirs, directions = interp_t.shape
    split = share % 16 == 0
    near = near.reshape(2, parents, 8, unknowns, columns)
    receive = receive.reshape(parents, 8, 2, unknowns, leaf_dirs)
    if not split:
        incoming = jnp.transpose(incoming, (1, 2, 0, 3, 4)).reshape(2, parents, directions, columns)

    width = 2 * leaf_dirs

    def body(in_ref, near_ref, rec_ref, interp_ref, cos_ref, sin_ref, out_ref, shift_ref, arriving):
        @pl.when(pl.program_id(0) == 0)
        def _():
            wide = interp_ref[...].astype(jnp.float32)
            for c in range(8):
                real = (wide * cos_ref[c : c + 1, :]).astype(jnp.bfloat16)
                imag = (wide * sin_ref[c : c + 1, :]).astype(jnp.bfloat16)
                shift_ref[c * width : (c + 1) * width, :] = complex_matrix(real, -imag)

        pieces = [
            in_ref[:, part, 0].reshape(directions, columns) if split else in_ref[part, 0]
            for part in range(2)
        ]
        source = jnp.concatenate(pieces, axis=0)
        arriving[...] = dot(shift_ref[...], source).astype(jnp.bfloat16)
        for c in range(8):
            mat = complex_matrix(rec_ref[0, c, 0], rec_ref[0, c, 1])
            far = dot(mat, arriving[c * width : (c + 1) * width, :])
            for part in range(2):
                total = near_ref[part, 0, c].astype(jnp.float32)
                total = total + far[part * unknowns : (part + 1) * unknowns]
                out_ref[part, 0, c] = total.astype(jnp.bfloat16)

    if split:
        in_spec = pl.BlockSpec((parts, 2, 1, share, columns), lambda p: (0, 0, p, 0, 0))
    else:
        in_spec = pl.BlockSpec((2, 1, directions, columns), lambda p: (0, p, 0, 0))
    out = pl.pallas_call(
        body,
        grid=(parents,),
        in_specs=[
            in_spec,
            pl.BlockSpec((2, 1, 8, unknowns, columns), lambda p: (0, p, 0, 0, 0)),
            pl.BlockSpec((1, 8, 2, unknowns, leaf_dirs), lambda p: (p, 0, 0, 0, 0)),
            pl.BlockSpec((leaf_dirs, directions), lambda p: (0, 0)),
            pl.BlockSpec((8, directions), lambda p: (0, 0)),
            pl.BlockSpec((8, directions), lambda p: (0, 0)),
        ],
        out_specs=pl.BlockSpec((2, 1, 8, unknowns, columns), lambda p: (0, p, 0, 0, 0)),
        out_shape=jax.ShapeDtypeStruct(near.shape, jnp.bfloat16),
        scratch_shapes=[
            pltpu.VMEM((8 * width, 2 * directions), jnp.bfloat16),
            pltpu.VMEM((8 * width, columns), jnp.bfloat16),
        ],
        compiler_params=pltpu.CompilerParams(vmem_limit_bytes=VMEM_BYTES),
        name="downward",
    )(incoming, near, receive, interp_t, cosine, sine)
    return out.reshape(2, boxes, unknowns, columns)


def local(
    currents,
    near_tiles,
    near_index,
    near_count,
    radiate,
    receive,
    interp,
    shift_angle,
    far_index,
    far_count,
    trans_index,
    translators,
):
    boxes = currents.shape[1]
    reach = boxes // 2
    parts = lax.axis_size(AXES)
    lower = [passed_along(currents[part, boxes - reach :], AXES, 1) for part in range(2)]
    upper = [passed_along(currents[part, :reach], AXES, -1) for part in range(2)]
    cosine = jnp.cos(shift_angle)
    sine = jnp.sin(shift_angle)
    parent = upward(currents, radiate, interp, cosine, sine, parts)
    parent, lower[0], upper[0], far_index, trans_index, translators = lax.optimization_barrier(
        (parent, lower[0], upper[0], far_index, trans_index, translators)
    )
    by_direction = lax.all_to_all(parent, AXES, split_axis=0, concat_axis=0, tiled=True)
    matrix = wire_matrix(
        translation_matrix(far_index, far_count, trans_index, translators), parts
    )
    first = lax.axis_index(AXES) * boxes - reach
    by_direction, lower[1], upper[1] = lax.optimization_barrier((by_direction, lower[1], upper[1]))
    translated = translate(by_direction, matrix)
    translated, near_count = lax.optimization_barrier((translated, near_count))
    near = near_products(lower, currents, upper, near_tiles, near_index, near_count, first)
    incoming = lax.all_to_all(translated, AXES, split_axis=0, concat_axis=0, tiled=True)
    return downward(incoming, near, receive, interp.T, cosine, sine)


def solution(mesh):
    placed = (
        P(None, ("box", "dir"), None, None),
        P(("box", "dir"), None, None, None, None),
        P(("box", "dir"), None),
        P(("box", "dir")),
        P(("box", "dir"), None, None, None),
        P(("box", "dir"), None, None, None),
        P(),
        P(),
        P(),
        P(),
        P(),
        P(None, None, ("box", "dir")),
    )
    return jax.shard_map(
        local,
        mesh=mesh,
        in_specs=placed,
        out_specs=P(None, ("box", "dir"), None, None),
        check_vma=False,
    )
```
